256 devices in a mesh: dp: 256 (over x, z, y, core).
Axes of the slice: x: 4, y: 4, z: 8, core: 2. Of those that a mesh axis runs over, the one named last changes fastest.
Arguments:
- picture_embedding_unscaled: bfloat16 [262144, 1152], P('dp'), may hold values from -6 to 6
- caption_embedding_unscaled: bfloat16 [262144, 1152], P('dp'), may hold values from -6 to 6
- score_multiplier: float32 [1], replicated, may hold values from 5 to 15
- score_shift_term_array: float32 [1], replicated, may hold values from -4 to -1
Outputs:
- row_loss: float32 [262144], P('dp')
- image_grad: bfloat16 [262144, 1152], P('dp')
- text_grad: bfloat16 [262144, 1152], P('dp')
The draws below stay inside these ranges and needn't reach their ends.
All inputs are finite; a program needn't handle non-finite values.
Results may differ from the reference program's by a relative error of at most 0.0061.
Values may be sent and summed in bfloat16 or wider, within the bound.
A program may use at most 64 MiB of HBM per device.

```python
import math
import jax
import jax.numpy as jnp
from jax import lax

D = 1152
B_DEV = 1024
ROUNDS = 2
BATCH = 262144
N_DP = 256


def steps_of(stream_key, shape, pieces, least, high):
    factor_of = 1.0
    for position, blocks in pieces:
        steps = jax.random.uniform(jax.random.fold_in(jax.random.fold_in(stream_key, 6), position), (blocks,), jnp.float32, least / len(pieces), high / len(pieces))
        factor_of = factor_of * jnp.repeat(jnp.exp(steps), shape[position] // blocks).reshape((-1,) + (1,) * (len(shape) - 1 - position))
    return factor_of


def bell_draw(stream_key, dims, spread, limit, pieces=(), kind=jnp.bfloat16):
    result = spread * jax.random.normal(stream_key, dims, jnp.float32)
    if pieces:
        result = result * steps_of(stream_key, dims, pieces, -0.22, 0.18)
    return jnp.clip(result, -limit, limit).astype(kind)


def setup_inputs(seed: int = 0) -> dict:
    streams_of = jax.random.split(jax.random.key(seed), 5)
    return {
        "picture_embedding_unscaled": bell_draw(streams_of[0], (BATCH, D), 1.0, 6.0, ((0, 256),)),
        "caption_embedding_unscaled": bell_draw(streams_of[1], (BATCH, D), 1.0, 6.0, ((0, 256),)),
        "score_multiplier": jnp.clip(jnp.exp(jax.random.uniform(streams_of[2], (1,), jnp.float32, math.log(5.0), math.log(15.0))), 5.0, 15.0),
        "score_shift_term_array": jnp.clip(jax.random.uniform(streams_of[3], (1,), jnp.float32, -4.0, -1.0), -4.0, -1.0),
    }


def normalize(values):
    wide = values.astype(jnp.float32)
    size = jnp.sqrt(lax.optimization_barrier(jnp.sum(wide * wide, axis=-1, keepdims=True)) + 1e-06)
    return (wide / size, size)

def tile_penalty_parts(preceding_device, following_device, score_multiplier, score_shift_term_array, matched_entry_filter):
    inner_similarity = jnp.einsum('id,jd->ij', preceding_device.astype(jnp.float32), following_device.astype(jnp.float32))
    couple_scores = score_multiplier[0] * inner_similarity + score_shift_term_array[0]
    target_polarity = jnp.where(matched_entry_filter, 1.0, -1.0).astype(jnp.float32)
    loss_values = lax.optimization_barrier(jnp.sum(jax.nn.softplus(-target_polarity * couple_scores), axis=1))
    derivative_multiplier = (-target_polarity * jax.nn.sigmoid(-target_polarity * couple_scores) * score_multiplier[0]).astype(jnp.bfloat16)
    return (loss_values, derivative_multiplier)

def unit_backward(grad, unit, size):
    along = lax.optimization_barrier(jnp.sum(unit * grad, axis=-1, keepdims=True))
    return ((grad - unit * along) / size).astype(jnp.bfloat16)

def reference(picture_embedding_unscaled, caption_embedding_unscaled, score_multiplier, score_shift_term_array):
    image_unit, image_size = normalize(picture_embedding_unscaled)
    text_unit, text_size = normalize(caption_embedding_unscaled)
    picture_summed_share = image_unit.astype(jnp.bfloat16).reshape(N_DP, B_DEV, D)
    caption_summed_share = text_unit.astype(jnp.bfloat16).reshape(N_DP, B_DEV, D)
    identity = jnp.eye(B_DEV, dtype=bool)
    loss_values = jnp.zeros((N_DP, B_DEV), jnp.float32)
    image_acc = jnp.zeros((N_DP, B_DEV, D), jnp.float32)
    text_acc = jnp.zeros((N_DP, B_DEV, D), jnp.float32)
    for step in range(ROUNDS):
        counterpart_slice = jnp.roll(caption_summed_share, step, axis=0)
        matched_entry_filter = identity if step == 0 else jnp.zeros_like(identity)

        def meeting(pair):
            preceding_device, following_device = pair
            line_penalty_parts, derivative_multiplier = tile_penalty_parts(preceding_device, following_device, score_multiplier, score_shift_term_array, matched_entry_filter)
            wide = derivative_multiplier.astype(jnp.float32)
            left_grad = jnp.einsum('ij,jd->id', wide, following_device.astype(jnp.float32))
            right_grad = jnp.einsum('ij,id->jd', wide, preceding_device.astype(jnp.float32))
            return (line_penalty_parts, left_grad, right_grad)
        line_penalty_parts, left_grad, right_grad = lax.map(meeting, (picture_summed_share, counterpart_slice))
        loss_values = loss_values + line_penalty_parts
        image_acc = image_acc + left_grad
        if step > 0:
            right_grad = lax.optimization_barrier(right_grad.astype(jnp.bfloat16)).astype(jnp.float32)
        text_acc = text_acc + jnp.roll(right_grad, -step, axis=0)
    row_loss = (loss_values / (ROUNDS * B_DEV)).reshape(-1)
    image_grad = unit_backward(image_acc.reshape(-1, D), image_unit, image_size)
    text_grad = unit_backward(text_acc.reshape(-1, D), text_unit, text_size)
    return (row_loss, image_grad, text_grad)
```

```python
import functools
import math

import jax
import jax.numpy as jnp
from jax import lax
from jax.experimental import pallas as pl
from jax.experimental.pallas import tpu as pltpu
from jax.sharding import PartitionSpec as P

ROUNDS = 2
EPS = 1e-06
LOG2E = 1.0 / math.log(2.0)
LN2 = math.log(2.0)
TILE = 256
MESH = pl.DeviceIdType.MESH
F32 = jnp.float32
BF16 = jnp.bfloat16


def dot_nt(a, b):
    return lax.dot_general(a, b, (((1,), (1,)), ((), ())), preferred_element_type=F32)


def dot_nn(a, b):
    return lax.dot_general(a, b, (((1,), (0,)), ((), ())), preferred_element_type=F32)


def softplus_and_coeff(exponent, scale):
    e = jnp.exp2(exponent)
    one = 1.0 + e
    small = e * (1.0 - e * (0.5 - e * (1.0 / 3.0)))
    loss = jnp.where(e < 0.002, small, jnp.log(one))
    coeff = (e / one) * scale
    return loss, coeff


def lane_groups(x):
    total = x[:, :128]
    for k in range(1, x.shape[1] // 128):
        total = total + x[:, k * 128 : (k + 1) * 128]
    return total


def sublane_groups(x):
    return jnp.sum(x.reshape(x.shape[0] // 8, 8, x.shape[1]), axis=0)


def normalize_rows(raw, low, inv, rows):
    x = raw[rows, :].astype(F32)
    size = jnp.sqrt(jnp.sum(x * x, axis=-1, keepdims=True) + EPS)
    recip = 1.0 / size
    low[rows, :] = (x * recip).astype(BF16)
    inv[rows, :] = jnp.broadcast_to(recip, (recip.shape[0], 128))


def project(grad, raw, inv, rows):
    recip = inv[rows, :][:, :1]
    unit = raw[rows, :].astype(F32) * recip
    along = jnp.sum(unit * grad, axis=-1, keepdims=True)
    return ((grad - unit * along) * recip).astype(BF16)


def pair_kernel(
    img, txt, scale_ref, shift_ref,
    loss_o, ga_o, gb_o,
    ar, br, al, bl, ys, yf, ct, da, ainv, binv, la, lb, lcol,
    lsa, lsb, ssend, srecv, fsend, frecv,
):
    pairs = ar.shape[0]
    nt = pairs // TILE
    me = lax.axis_index("dp")
    n = lax.axis_size("dp")
    parity = lax.rem(me, 2)
    slow = lax.rem(me + n - 1 + 2 * parity, n)
    fast = me + 1 - 2 * parity

    barrier = pltpu.get_barrier_semaphore()
    for partner in (slow, fast):
        pl.semaphore_signal(barrier, inc=1, device_id=(partner,), device_id_type=MESH)

    def chunk(i):
        return pl.ds(i * TILE, TILE)

    def load(src, dst, sem, i):
        return pltpu.make_async_copy(src.at[chunk(i)], dst.at[chunk(i)], sem.at[i])

    def send_slow(i):
        return pltpu.make_async_remote_copy(
            al.at[chunk(i)], ys.at[chunk(i)], ssend.at[i], srecv.at[i], (slow,), MESH
        )

    def send_fast(i):
        return pltpu.make_async_remote_copy(
            bl.at[chunk(i)], yf.at[chunk(i)], fsend.at[i], frecv.at[i], (fast,), MESH
        )

    @pl.when(parity == 0)
    def _():
        for i in range(nt):
            load(img, ar, lsa, i).start()
        for i in range(nt):
            load(txt, br, lsb, i).start()

    @pl.when(parity == 1)
    def _():
        for i in range(nt):
            load(txt, ar, lsa, i).start()
        for i in range(nt):
            load(img, br, lsb, i).start()

    for i in range(nt):
        load(img, ar, lsa, i).wait()
        normalize_rows(ar, al, ainv, chunk(i))
    pl.semaphore_wait(barrier, 2)
    for i in range(nt):
        send_slow(i).start()
    for i in range(nt):
        load(img, br, lsb, i).wait()
        normalize_rows(br, bl, binv, chunk(i))
        send_fast(i).start()

    lcol[...] = jnp.zeros_like(lcol)
    scale = scale_ref[0]
    scale2 = scale * LOG2E
    shift2 = shift_ref[0] * LOG2E

    for i in range(nt):
        rows = chunk(i)
        exponent = dot_nt(al[rows, :], bl[...]) * scale2 + shift2
        r = lax.broadcasted_iota(jnp.int32, exponent.shape, 0) + i * TILE
        c = lax.broadcasted_iota(jnp.int32, exponent.shape, 1)
        match = r == c
        exponent = jnp.where(match, -exponent, exponent)
        loss, coeff = softplus_and_coeff(exponent, jnp.where(match, -scale, scale))
        la[rows, :] = lane_groups(loss)
        lcol[...] += sublane_groups(loss)
        low = coeff.astype(BF16)
        ct[:, rows] = low.T
        da[rows, :] = dot_nn(low, bl[...])

    for i in range(nt):
        send_fast(i).wait_recv()

    for j in range(nt):
        rows = chunk(j)
        exponent = dot_nt(bl[rows, :], yf[...]) * scale2 + shift2
        loss, coeff = softplus_and_coeff(exponent, scale)
        lb[rows, :] = lane_groups(loss)
        grad = dot_nn(ct[rows, :], al[...]) + dot_nn(coeff.astype(BF16), yf[...])
        gb_o[rows, :] = project(grad, br, binv, rows)

    for c in range(nt):
        send_slow(c).wait_recv()

        block = ys[chunk(c), :]
        for i in range(nt):
            rows = chunk(i)
            exponent = dot_nt(al[rows, :], block) * scale2 + shift2
            loss, coeff = softplus_and_coeff(exponent, scale)
            la[rows, :] += lane_groups(loss)
            grad = da[rows, :] + dot_nn(coeff.astype(BF16), block)
            if c < nt - 1:
                da[rows, :] = grad
            else:
                ga_o[rows, :] = project(grad, ar, ainv, rows)

    mean = 1.0 / (ROUNDS * pairs)

    @pl.when(parity == 0)
    def _():
        for k in range(pairs // 128):
            block = la[k * 128 : (k + 1) * 128, :].T
            loss_o[k : k + 1, :] = jnp.sum(block, axis=0, keepdims=True) * mean

    @pl.when(parity == 1)
    def _():
        for k in range(pairs // 128):
            block = lb[k * 128 : (k + 1) * 128, :].T
            own = jnp.sum(lcol[:, k * 128 : (k + 1) * 128], axis=0, keepdims=True)
            loss_o[k : k + 1, :] = (jnp.sum(block, axis=0, keepdims=True) + own) * mean

    for i in range(nt):
        send_fast(i).wait_send()
    for i in range(nt):
        send_slow(i).wait_send()


def place_kernel(loss, ga, gb, loss_o, gimg_o, gtxt_o, sems):
    parity = lax.rem(lax.axis_index("dp"), 2)

    @pl.when(parity == 0)
    def _():
        pltpu.make_async_copy(ga, gimg_o, sems.at[0]).start()
        pltpu.make_async_copy(gb, gtxt_o, sems.at[1]).start()

    @pl.when(parity == 1)
    def _():
        pltpu.make_async_copy(gb, gimg_o, sems.at[0]).start()
        pltpu.make_async_copy(ga, gtxt_o, sems.at[1]).start()

    last = pltpu.make_async_copy(loss, loss_o, sems.at[2])
    last.start()
    pltpu.make_async_copy(ga, gimg_o, sems.at[0]).wait()
    pltpu.make_async_copy(gb, gtxt_o, sems.at[1]).wait()
    last.wait()


def shards(img, txt, scale, shift):
    pairs, width = img.shape
    nt = pairs // TILE
    hbm_spec = pl.BlockSpec(memory_space=pltpu.HBM)
    smem_spec = pl.BlockSpec(memory_space=pltpu.SMEM)
    vmem_spec = pl.BlockSpec(memory_space=pltpu.VMEM)
    block = pltpu.VMEM((pairs, width), BF16)
    loss, ga, gb = pl.pallas_call(
        pair_kernel,
        out_shape=(
            pltpu.VMEM((pairs // 128, 128), F32),
            pltpu.VMEM((pairs, width), BF16),
            pltpu.VMEM((pairs, width), BF16),
        ),
        in_specs=[hbm_spec, hbm_spec, smem_spec, smem_spec],
        out_specs=(vmem_spec, vmem_spec, vmem_spec),
        scratch_shapes=[
            block, block, block, block, block, block,
            pltpu.VMEM((pairs, pairs), BF16),
            pltpu.VMEM((pairs, width), F32),
            pltpu.VMEM((pairs, 128), F32),
            pltpu.VMEM((pairs, 128), F32),
            pltpu.VMEM((pairs, 128), F32),
            pltpu.VMEM((pairs, 128), F32),
            pltpu.VMEM((8, pairs), F32),
        ]
        + [pltpu.SemaphoreType.DMA((nt,))] * 6,
        compiler_params=pltpu.CompilerParams(
            collective_id=0, has_side_effects=True, vmem_limit_bytes=44 * 2**20
        ),
        name="pair_tiles",
    )(
        pltpu.with_memory_space_constraint(img, pltpu.HBM),
        pltpu.with_memory_space_constraint(txt, pltpu.HBM),
        scale,
        shift,
    )
    loss, gimg, gtxt = pl.pallas_call(
        place_kernel,
        out_shape=(
            jax.ShapeDtypeStruct(loss.shape, F32),
            jax.ShapeDtypeStruct(img.shape, BF16),
            jax.ShapeDtypeStruct(txt.shape, BF16),
        ),
        in_specs=[vmem_spec] * 3,
        out_specs=(hbm_spec, hbm_spec, hbm_spec),
        scratch_shapes=[pltpu.SemaphoreType.DMA((3,))],
        compiler_params=pltpu.CompilerParams(vmem_limit_bytes=2**20),
        name="place_outputs",
    )(*(pltpu.with_memory_space_constraint(x, pltpu.VMEM) for x in (loss, ga, gb)))
    return loss.reshape(pairs), gimg, gtxt


def solution(mesh):
    in_specs = (P("dp", None), P("dp", None), P(), P())
    out_specs = (P("dp"), P("dp", None), P("dp", None))
    return jax.shard_map(shards, mesh=mesh, in_specs=in_specs, out_specs=out_specs, check_vma=False)
```

```python
import functools
import math

import jax
import jax.numpy as jnp
from jax import lax
from jax.experimental import pallas as pl
from jax.experimental.pallas import tpu as pltpu
from jax.sharding import PartitionSpec as P

ROUNDS = 2
EPS = 1e-06
LOG2E = 1.0 / math.log(2.0)
LN2 = math.log(2.0)
TILE = 256
SLOW_CHUNKS = ((0, 768), (768, 256))
LATE_EVERY = 64
LATE_TILE = 1
MESH = pl.DeviceIdType.MESH
F32 = jnp.float32
BF16 = jnp.bfloat16


def dot_nt(a, b):
    return lax.dot_general(a, b, (((1,), (1,)), ((), ())), preferred_element_type=F32)


def dot_nn(a, b):
    return lax.dot_general(a, b, (((1,), (0,)), ((), ())), preferred_element_type=F32)


def softplus_and_coeff(exponent, scale):
    e = jnp.exp2(exponent)
    one = 1.0 + e
    small = e * (1.0 - e * (0.5 - e * (1.0 / 3.0)))
    loss = jnp.where(e < 0.002, small, jnp.log(one))
    coeff = (e / one) * scale
    return loss, coeff


def lane_groups(x):
    total = x[:, :128]
    for k in range(1, x.shape[1] // 128):
        total = total + x[:, k * 128 : (k + 1) * 128]
    return total


def sublane_groups(x):
    return jnp.sum(x.reshape(x.shape[0] // 8, 8, x.shape[1]), axis=0)


def inverse_size(x):
    return 1.0 / jnp.sqrt(jnp.sum(x * x, axis=-1, keepdims=True) + EPS)


def row_of(partial, k):
    return jnp.sum(partial[k * 128 : (k + 1) * 128, :].T, axis=0, keepdims=True)


def normalize_rows(raw, low, rows, inv=None):
    x = raw[rows, :].astype(F32)
    recip = inverse_size(x)
    low[rows, :] = (x * recip).astype(BF16)
    if inv is not None:
        inv[rows, :] = jnp.broadcast_to(recip, (recip.shape[0], 128))


def project(grad, raw, inv, rows):
    recip = inv[rows, :][:, :1]
    unit = raw[rows, :].astype(F32) * recip
    along = jnp.sum(unit * grad, axis=-1, keepdims=True)
    return ((grad - unit * along) * recip).astype(BF16)


def pair_kernel(
    img, txt, scale_ref, shift_ref,
    odd_loss, gb_o, la, da, ar, al, ainv, last_low,
    br, bl, yr, ys, yf, ct, binv, lb, lcol,
    lsa, lsb, ssend, srecv, fsend, frecv,
):
    pairs = ar.shape[0]
    nt = pairs // TILE
    me = lax.axis_index("dp")
    n = lax.axis_size("dp")
    parity = lax.rem(me, 2)
    slow = lax.rem(me + n - 1 + 2 * parity, n)
    fast = me + 1 - 2 * parity

    barrier = pltpu.get_barrier_semaphore()
    for partner in (slow, fast):
        pl.semaphore_signal(barrier, inc=1, device_id=(partner,), device_id_type=MESH)

    def chunk(i):
        return pl.ds(i * TILE, TILE)

    def load(src, dst, sem, i):
        return pltpu.make_async_copy(src.at[chunk(i)], dst.at[chunk(i)], sem.at[i])

    def send_slow(i, src=img):
        return pltpu.make_async_remote_copy(
            src.at[pl.ds(*SLOW_CHUNKS[i])], yr.at[pl.ds(*SLOW_CHUNKS[i])], ssend.at[i], srecv.at[i], (slow,), MESH
        )

    def start_slow():
        @pl.when(parity == 0)
        def _():
            for i in range(len(SLOW_CHUNKS)):
                send_slow(i, img).start()

        @pl.when(parity == 1)
        def _():
            for i in range(len(SLOW_CHUNKS)):
                send_slow(i, txt).start()

    def send_fast(i):
        return pltpu.make_async_remote_copy(
            bl.at[chunk(i)], yf.at[chunk(i)], fsend.at[i], frecv.at[i], (fast,), MESH
        )

    @pl.when(parity == 0)
    def _():
        for i in range(nt):
            load(img, ar, lsa, i).start()
        for i in range(nt):
            load(txt, br, lsb, i).start()

    @pl.when(parity == 1)
    def _():
        for i in range(nt):
            load(txt, ar, lsa, i).start()
        for i in range(nt):
            load(img, br, lsb, i).start()

    late = lax.rem(me, LATE_EVERY) == 0

    @pl.when(jnp.logical_not(late))
    def _():
        pl.semaphore_wait(barrier, 2)
        start_slow()

    for i in range(nt):
        load(img, br, lsb, i).wait()
        normalize_rows(br, bl, chunk(i), binv)

    @pl.when(jnp.logical_not(late))
    def _():
        for i in range(nt):
            send_fast(i).start()

    for i in range(nt):
        load(img, ar, lsa, i).wait()
        normalize_rows(ar, al, chunk(i), ainv)

    lcol[...] = jnp.zeros_like(lcol)
    scale = scale_ref[0]
    scale2 = scale * LOG2E
    shift2 = shift_ref[0] * LOG2E

    for i in range(nt):
        rows = chunk(i)
        exponent = dot_nt(al[rows, :], bl[...]) * scale2 + shift2
        r = lax.broadcasted_iota(jnp.int32, exponent.shape, 0) + i * TILE
        c = lax.broadcasted_iota(jnp.int32, exponent.shape, 1)
        match = r == c
        exponent = jnp.where(match, -exponent, exponent)
        loss, coeff = softplus_and_coeff(exponent, jnp.where(match, -scale, scale))
        la[rows, :] = lane_groups(loss)
        lcol[...] += sublane_groups(loss)
        low = coeff.astype(BF16)
        ct[:, rows] = low.T
        da[rows, :] = dot_nn(low, bl[...])
        if i == LATE_TILE:

            @pl.when(late)
            def _():
                pl.semaphore_wait(barrier, 2)
                start_slow()
                for k in range(nt):
                    send_fast(k).start()


    for i in range(nt):
        send_fast(i).wait_recv()

    for j in range(nt):
        rows = chunk(j)
        exponent = dot_nt(bl[rows, :], yf[...]) * scale2 + shift2
        loss, coeff = softplus_and_coeff(exponent, scale)
        lb[rows, :] = lane_groups(loss)
        grad = dot_nn(ct[rows, :], al[...]) + dot_nn(coeff.astype(BF16), yf[...])
        gb_o[rows, :] = project(grad, br, binv, rows)

    mean = 1.0 / (ROUNDS * pairs)
    for k in range(pairs // 128):
        own = jnp.sum(lcol[:, k * 128 : (k + 1) * 128], axis=0, keepdims=True)
        odd_loss[k : k + 1, :] = (row_of(lb, k) + own) * mean

    for c, (first, count) in enumerate(SLOW_CHUNKS[:-1]):
        send_slow(c).wait_recv()
        part = pl.ds(first, count)
        normalize_rows(yr, ys, part)
        block = ys[part, :]
        for i in range(nt):
            rows = chunk(i)
            exponent = dot_nt(al[rows, :], block) * scale2 + shift2
            loss, coeff = softplus_and_coeff(exponent, scale)
            la[rows, :] += lane_groups(loss)
            da[rows, :] += dot_nn(coeff.astype(BF16), block)

    send_slow(len(SLOW_CHUNKS) - 1).wait_recv()
    last_rows = yr[pl.ds(*SLOW_CHUNKS[-1]), :].astype(F32)
    last_low[...] = (last_rows * inverse_size(last_rows)).astype(BF16)

    for i in range(nt):
        send_fast(i).wait_send()
    for i in range(len(SLOW_CHUNKS)):
        send_slow(i).wait_send()


def last_kernel(
    scale_ref, shift_ref, odd_loss, gb, la, da, ar, al, ainv, last_low,
    loss_o, gimg_o, gtxt_o,
    ga, rows_loss, sems,
):
    parity = lax.rem(lax.axis_index("dp"), 2)
    pairs = ga.shape[0]
    nt = pairs // TILE

    def place(src, dst, which, k):
        rows = pl.ds(k * TILE, TILE)
        return pltpu.make_async_copy(src.at[rows], dst.at[rows], sems.at[which, k])

    @pl.when(parity == 0)
    def _():
        for k in range(nt):
            place(gb, gtxt_o, 1, k).start()

    @pl.when(parity == 1)
    def _():
        for k in range(nt):
            place(gb, gimg_o, 1, k).start()

    scale = scale_ref[0]
    scale2 = scale * LOG2E
    shift2 = shift_ref[0] * LOG2E
    block = last_low[...]
    mean = 1.0 / (ROUNDS * pairs)
    lows = []
    for i in range(nt):
        rows = pl.ds(i * TILE, TILE)
        exponent = dot_nt(al[rows, :], block) * scale2 + shift2
        loss, coeff = softplus_and_coeff(exponent, scale)
        lows.append(coeff.astype(BF16))
        total = la[rows, :] + lane_groups(loss)
        for h in range(TILE // 128):
            k = i * (TILE // 128) + h
            even = row_of(total, h) * mean
            rows_loss[k : k + 1, :] = jnp.where(parity == 0, even, odd_loss[k : k + 1, :])
    loss_copy = pltpu.make_async_copy(rows_loss, loss_o, sems.at[2, 0])
    loss_copy.start()

    def start_place(k):
        @pl.when(parity == 0)
        def _():
            place(ga, gimg_o, 0, k).start()

        @pl.when(parity == 1)
        def _():
            place(ga, gtxt_o, 0, k).start()

    for i in range(nt):
        rows = pl.ds(i * TILE, TILE)
        grad = da[rows, :] + dot_nn(lows[i], block)
        ga[rows, :] = project(grad, ar, ainv, rows)
        start_place(i)

    for k in range(nt):
        place(ga, gimg_o, 0, k).wait()
        place(gb, gtxt_o, 1, k).wait()
    loss_copy.wait()


def shards(img, txt, scale, shift):
    pairs, width = img.shape
    nt = pairs // TILE
    hbm_spec = pl.BlockSpec(memory_space=pltpu.HBM)
    smem_spec = pl.BlockSpec(memory_space=pltpu.SMEM)
    vmem_spec = pl.BlockSpec(memory_space=pltpu.VMEM)
    block = pltpu.VMEM((pairs, width), BF16)
    partial = pltpu.VMEM((pairs, 128), F32)
    held = pl.pallas_call(
        pair_kernel,
        out_shape=(
            pltpu.VMEM((pairs // 128, 128), F32),
            block,
            partial,
            pltpu.VMEM((pairs, width), F32),
            block,
            block,
            partial,
            pltpu.VMEM((SLOW_CHUNKS[-1][1], width), BF16),
        ),
        in_specs=[hbm_spec, hbm_spec, smem_spec, smem_spec],
        out_specs=(vmem_spec,) * 8,
        scratch_shapes=[
            block, block, block, block, block,
            pltpu.VMEM((pairs, pairs), BF16),
            partial,
            partial,
            pltpu.VMEM((8, pairs), F32),
        ]
        + [pltpu.SemaphoreType.DMA((nt,))] * 2
        + [pltpu.SemaphoreType.DMA((len(SLOW_CHUNKS),))] * 2
        + [pltpu.SemaphoreType.DMA((nt,))] * 2,
        compiler_params=pltpu.CompilerParams(
            collective_id=0, has_side_effects=True, vmem_limit_bytes=32 * 2**20
        ),
        name="pair_tiles",
    )(
        pltpu.with_memory_space_constraint(img, pltpu.HBM),
        pltpu.with_memory_space_constraint(txt, pltpu.HBM),
        scale,
        shift,
    )
    loss, gimg, gtxt = pl.pallas_call(
        last_kernel,
        out_shape=(
            jax.ShapeDtypeStruct((pairs // 128, 128), F32),
            jax.ShapeDtypeStruct(img.shape, BF16),
            jax.ShapeDtypeStruct(txt.shape, BF16),
        ),
        in_specs=[smem_spec, smem_spec] + [vmem_spec] * 8,
        out_specs=(hbm_spec, hbm_spec, hbm_spec),
        scratch_shapes=[
            block,
            pltpu.VMEM((pairs // 128, 128), F32),
            pltpu.SemaphoreType.DMA((3, nt)),
        ],
        compiler_params=pltpu.CompilerParams(vmem_limit_bytes=16 * 2**20),
        name="last_tiles",
    )(scale, shift, *(pltpu.with_memory_space_constraint(x, pltpu.VMEM) for x in held))
    return loss.reshape(pairs), gimg, gtxt


def solution(mesh):
    in_specs = (P("dp", None), P("dp", None), P(), P())
    out_specs = (P("dp"), P("dp", None), P("dp", None))
    return jax.shard_map(shards, mesh=mesh, in_specs=in_specs, out_specs=out_specs, check_vma=False)
```

```python
import functools
import math

import jax
import jax.numpy as jnp
from jax import lax
from jax.experimental import pallas as pl
from jax.experimental.pallas import tpu as pltpu
from jax.sharding import PartitionSpec as P

ROUNDS = 2
EPS = 1e-06
LOG2E = 1.0 / math.log(2.0)
LN2 = math.log(2.0)
TILE = 256
SLOW_CHUNKS = ((0, 640), (640, 256), (896, 128))
LATE_EVERY = 64
LATE_TILE = 1
MESH = pl.DeviceIdType.MESH
F32 = jnp.float32
BF16 = jnp.bfloat16


def dot_nt(a, b):
    return lax.dot_general(a, b, (((1,), (1,)), ((), ())), preferred_element_type=F32)


def dot_nn(a, b):
    return lax.dot_general(a, b, (((1,), (0,)), ((), ())), preferred_element_type=F32)


def softplus_and_coeff(exponent, scale):
    e = jnp.exp2(exponent)
    one = 1.0 + e
    small = e * (1.0 - e * (0.5 - e * (1.0 / 3.0)))
    loss = jnp.where(e < 0.002, small, jnp.log(one))
    coeff = (e / one) * scale
    return loss, coeff


def lane_groups(x):
    total = x[:, :128]
    for k in range(1, x.shape[1] // 128):
        total = total + x[:, k * 128 : (k + 1) * 128]
    return total


def sublane_groups(x):
    return jnp.sum(x.reshape(x.shape[0] // 8, 8, x.shape[1]), axis=0)


def inverse_size(x):
    return 1.0 / jnp.sqrt(jnp.sum(x * x, axis=-1, keepdims=True) + EPS)


def row_of(partial, k):
    return jnp.sum(partial[k * 128 : (k + 1) * 128, :].T, axis=0, keepdims=True)


def normalize_rows(raw, low, rows, inv=None):
    x = raw[rows, :].astype(F32)
    recip = inverse_size(x)
    low[rows, :] = (x * recip).astype(BF16)
    if inv is not None:
        inv[rows, :] = jnp.broadcast_to(recip, (recip.shape[0], 128))


def project(grad, raw, inv, rows):
    recip = inv[rows, :][:, :1]
    unit = raw[rows, :].astype(F32) * recip
    along = jnp.sum(unit * grad, axis=-1, keepdims=True)
    return ((grad - unit * along) * recip).astype(BF16)


def pair_kernel(
    img, txt, scale_ref, shift_ref,
    odd_loss, gb_o, la, da, ar, al, ainv, last_low,
    br, bl, yr, ys, yf, ct, binv, lb, lcol,
    lsa, lsb, ssend, srecv, fsend, frecv,
):
    pairs = ar.shape[0]
    nt = pairs // TILE
    me = lax.axis_index("dp")
    n = lax.axis_size("dp")
    parity = lax.rem(me, 2)
    slow = lax.rem(me + n - 1 + 2 * parity, n)
    fast = me + 1 - 2 * parity

    barrier = pltpu.get_barrier_semaphore()
    for partner in (slow, fast):
        pl.semaphore_signal(barrier, inc=1, device_id=(partner,), device_id_type=MESH)

    def chunk(i):
        return pl.ds(i * TILE, TILE)

    def load(src, dst, sem, i):
        return pltpu.make_async_copy(src.at[chunk(i)], dst.at[chunk(i)], sem.at[i])

    def send_slow(i, src=img):
        return pltpu.make_async_remote_copy(
            src.at[pl.ds(*SLOW_CHUNKS[i])], yr.at[pl.ds(*SLOW_CHUNKS[i])], ssend.at[i], srecv.at[i], (slow,), MESH
        )

    def start_slow():
        @pl.when(parity == 0)
        def _():
            for i in range(len(SLOW_CHUNKS)):
                send_slow(i, img).start()

        @pl.when(parity == 1)
        def _():
            for i in range(len(SLOW_CHUNKS)):
                send_slow(i, txt).start()

    def send_fast(i):
        return pltpu.make_async_remote_copy(
            bl.at[chunk(i)], yf.at[chunk(i)], fsend.at[i], frecv.at[i], (fast,), MESH
        )

    @pl.when(parity == 0)
    def _():
        for i in range(nt):
            load(img, ar, lsa, i).start()
        for i in range(nt):
            load(txt, br, lsb, i).start()

    @pl.when(parity == 1)
    def _():
        for i in range(nt):
            load(txt, ar, lsa, i).start()
        for i in range(nt):
            load(img, br, lsb, i).start()

    late = lax.rem(me, LATE_EVERY) == 0

    @pl.when(jnp.logical_not(late))
    def _():
        pl.semaphore_wait(barrier, 2)
        start_slow()

    for i in range(nt):
        load(img, br, lsb, i).wait()
        normalize_rows(br, bl, chunk(i), binv)

    @pl.when(jnp.logical_not(late))
    def _():
        for i in range(nt):
            send_fast(i).start()

    for i in range(nt):
        load(img, ar, lsa, i).wait()
        normalize_rows(ar, al, chunk(i), ainv)

    lcol[...] = jnp.zeros_like(lcol)
    scale = scale_ref[0]
    scale2 = scale * LOG2E
    shift2 = shift_ref[0] * LOG2E

    for i in range(nt):
        rows = chunk(i)
        exponent = dot_nt(al[rows, :], bl[...]) * scale2 + shift2
        r = lax.broadcasted_iota(jnp.int32, exponent.shape, 0) + i * TILE
        c = lax.broadcasted_iota(jnp.int32, exponent.shape, 1)
        match = r == c
        exponent = jnp.where(match, -exponent, exponent)
        loss, coeff = softplus_and_coeff(exponent, jnp.where(match, -scale, scale))
        la[rows, :] = lane_groups(loss)
        lcol[...] += sublane_groups(loss)
        low = coeff.astype(BF16)
        ct[:, rows] = low.T
        da[rows, :] = dot_nn(low, bl[...])
        if i == LATE_TILE:

            @pl.when(late)
            def _():
                pl.semaphore_wait(barrier, 2)
                start_slow()
                for k in range(nt):
                    send_fast(k).start()


    for i in range(nt):
        send_fast(i).wait_recv()

    for j in range(nt):
        rows = chunk(j)
        exponent = dot_nt(bl[rows, :], yf[...]) * scale2 + shift2
        loss, coeff = softplus_and_coeff(exponent, scale)
        lb[rows, :] = lane_groups(loss)
        grad = dot_nn(ct[rows, :], al[...]) + dot_nn(coeff.astype(BF16), yf[...])
        gb_o[rows, :] = project(grad, br, binv, rows)

    mean = 1.0 / (ROUNDS * pairs)
    for k in range(pairs // 128):
        own = jnp.sum(lcol[:, k * 128 : (k + 1) * 128], axis=0, keepdims=True)
        odd_loss[k : k + 1, :] = (row_of(lb, k) + own) * mean

    for c, (first, count) in enumerate(SLOW_CHUNKS[:-1]):
        send_slow(c).wait_recv()
        part = pl.ds(first, count)
        normalize_rows(yr, ys, part)
        block = ys[part, :]
        for i in range(nt):
            rows = chunk(i)
            exponent = dot_nt(al[rows, :], block) * scale2 + shift2
            loss, coeff = softplus_and_coeff(exponent, scale)
            la[rows, :] += lane_groups(loss)
            da[rows, :] += dot_nn(coeff.astype(BF16), block)

    send_slow(len(SLOW_CHUNKS) - 1).wait_recv()
    last_rows = yr[pl.ds(*SLOW_CHUNKS[-1]), :].astype(F32)
    last_low[...] = (last_rows * inverse_size(last_rows)).astype(BF16)

    for i in range(nt):
        send_fast(i).wait_send()
    for i in range(len(SLOW_CHUNKS)):
        send_slow(i).wait_send()


def last_kernel(
    scale_ref, shift_ref, odd_loss, gb, la, da, ar, al, ainv, last_low,
    loss_o, gimg_o, gtxt_o,
    ga, rows_loss, sems,
):
    parity = lax.rem(lax.axis_index("dp"), 2)
    pairs = ga.shape[0]
    nt = pairs // TILE

    def place(src, dst, which, k):
        rows = pl.ds(k * TILE, TILE)
        return pltpu.make_async_copy(src.at[rows], dst.at[rows], sems.at[which, k])

    @pl.when(parity == 0)
    def _():
        for k in range(nt):
            place(gb, gtxt_o, 1, k).start()

    @pl.when(parity == 1)
    def _():
        for k in range(nt):
            place(gb, gimg_o, 1, k).start()

    scale = scale_ref[0]
    scale2 = scale * LOG2E
    shift2 = shift_ref[0] * LOG2E
    block = last_low[...]
    mean = 1.0 / (ROUNDS * pairs)
    lows = []
    for i in range(nt):
        rows = pl.ds(i * TILE, TILE)
        exponent = dot_nt(al[rows, :], block) * scale2 + shift2
        loss, coeff = softplus_and_coeff(exponent, scale)
        lows.append(coeff.astype(BF16))
        total = la[rows, :] + lane_groups(loss)
        for h in range(TILE // 128):
            k = i * (TILE // 128) + h
            even = row_of(total, h) * mean
            rows_loss[k : k + 1, :] = jnp.where(parity == 0, even, odd_loss[k : k + 1, :])
    loss_copy = pltpu.make_async_copy(rows_loss, loss_o, sems.at[2, 0])
    loss_copy.start()

    def start_place(k):
        @pl.when(parity == 0)
        def _():
            place(ga, gimg_o, 0, k).start()

        @pl.when(parity == 1)
        def _():
            place(ga, gtxt_o, 0, k).start()

    for i in range(nt):
        rows = pl.ds(i * TILE, TILE)
        grad = da[rows, :] + dot_nn(lows[i], block)
        ga[rows, :] = project(grad, ar, ainv, rows)
        start_place(i)

    for k in range(nt):
        place(ga, gimg_o, 0, k).wait()
        place(gb, gtxt_o, 1, k).wait()
    loss_copy.wait()


def shards(img, txt, scale, shift):
    pairs, width = img.shape
    nt = pairs // TILE
    hbm_spec = pl.BlockSpec(memory_space=pltpu.HBM)
    smem_spec = pl.BlockSpec(memory_space=pltpu.SMEM)
    vmem_spec = pl.BlockSpec(memory_space=pltpu.VMEM)
    block = pltpu.VMEM((pairs, width), BF16)
    partial = pltpu.VMEM((pairs, 128), F32)
    held = pl.pallas_call(
        pair_kernel,
        out_shape=(
            pltpu.VMEM((pairs // 128, 128), F32),
            block,
            partial,
            pltpu.VMEM((pairs, width), F32),
            block,
            block,
            partial,
            pltpu.VMEM((SLOW_CHUNKS[-1][1], width), BF16),
        ),
        in_specs=[hbm_spec, hbm_spec, smem_spec, smem_spec],
        out_specs=(vmem_spec,) * 8,
        scratch_shapes=[
            block, block, block, block, block,
            pltpu.VMEM((pairs, pairs), BF16),
            partial,
            partial,
            pltpu.VMEM((8, pairs), F32),
        ]
        + [pltpu.SemaphoreType.DMA((nt,))] * 2
        + [pltpu.SemaphoreType.DMA((len(SLOW_CHUNKS),))] * 2
        + [pltpu.SemaphoreType.DMA((nt,))] * 2,
        compiler_params=pltpu.CompilerParams(
            collective_id=0, has_side_effects=True, vmem_limit_bytes=32 * 2**20
        ),
        name="pair_tiles",
    )(
        pltpu.with_memory_space_constraint(img, pltpu.HBM),
        pltpu.with_memory_space_constraint(txt, pltpu.HBM),
        scale,
        shift,
    )
    loss, gimg, gtxt = pl.pallas_call(
        last_kernel,
        out_shape=(
            jax.ShapeDtypeStruct((pairs // 128, 128), F32),
            jax.ShapeDtypeStruct(img.shape, BF16),
            jax.ShapeDtypeStruct(txt.shape, BF16),
        ),
        in_specs=[smem_spec, smem_spec] + [vmem_spec] * 8,
        out_specs=(hbm_spec, hbm_spec, hbm_spec),
        scratch_shapes=[
            block,
            pltpu.VMEM((pairs // 128, 128), F32),
            pltpu.SemaphoreType.DMA((3, nt)),
        ],
        compiler_params=pltpu.CompilerParams(vmem_limit_bytes=16 * 2**20),
        name="last_tiles",
    )(scale, shift, *(pltpu.with_memory_space_constraint(x, pltpu.VMEM) for x in held))
    return loss.reshape(pairs), gimg, gtxt


def solution(mesh):
    in_specs = (P("dp", None), P("dp", None), P(), P())
    out_specs = (P("dp"), P("dp", None), P("dp", None))
    return jax.shard_map(shards, mesh=mesh, in_specs=in_specs, out_specs=out_specs, check_vma=False)
```
